32 devices in a mesh: crop: 1, row: 16 (over z, y, core), col: 2 (over x).
Axes of the slice: x: 2, y: 2, z: 4, core: 2. Of those that a mesh axis runs over, the one named last changes fastest.
Arguments:
- pair: bfloat16 [256, 256, 128], P(('crop', 'row'), 'col'), may hold values from -6 to 6
- norm_gain: float32 [128], replicated, may hold values from 0.1 to 1.9
- norm_bias: float32 [128], replicated, may hold values from -3 to 3
- left_weight: bfloat16 [128, 256], replicated, may hold values from -0.5 to 0.5
- right_weight: bfloat16 [128, 256], replicated, may hold values from -0.5 to 0.5
- gate_weight: bfloat16 [128, 128], replicated, may hold values from -0.5 to 0.5
- out_gain: float32 [128], replicated, may hold values from 0.1 to 1.9
- out_bias: float32 [128], replicated, may hold values from -3 to 3
- out_weight: bfloat16 [128, 128], replicated, may hold values from -0.5 to 0.5
Outputs:
- update: bfloat16 [256, 256, 128], P(('crop', 'row'), 'col')
The draws below stay inside these ranges and needn't reach their ends.
All inputs are finite; a program needn't handle non-finite values.
Results may differ from the reference program's by a relative error of at most 0.0085.
Values may be sent and summed in bfloat16 or wider, within the bound.
A program may use at most 64 MiB of HBM per device.

```python
import jax
import jax.numpy as jnp
from jax import lax

PAIR = 128
HIDDEN_SIZE = 128
TOK_ROW = 16
TOKENS = 256
N_ROW = 16


def levels(rng, dims, cuts, low, high):
    def one(axis_at, parts):
        draws = jax.random.uniform(jax.random.fold_in(jax.random.fold_in(rng, 6), axis_at), (parts,), jnp.float32, low / len(cuts), high / len(cuts))
        return jnp.repeat(jnp.exp(draws), dims[axis_at] // parts).reshape((-1,) + (1,) * (len(dims) - axis_at - 1))

    level = one(*cuts[0])
    for cut in cuts[1:]:
        level = level * one(*cut)
    return level


def normal_values(rng, dims, width, reach, split=(), kind=jnp.bfloat16):
    level = levels(rng, dims, split, -0.22, 0.18) if split else 1.0
    entries = jax.random.normal(rng, dims, jnp.float32) * width * level
    return jnp.minimum(jnp.maximum(entries, -reach), reach).astype(kind)


def setup_inputs(seed: int = 0, part: int = 0) -> dict:
    streams_of = jax.random.split(jax.random.key(seed), 10)
    part_keys = jax.random.split(jax.random.fold_in(streams_of[9], part), 10)
    pair = normal_values(part_keys[0], (TOKENS, TOKENS, PAIR), 1.0, 6.0, ((0, 16), (1, 2)))
    norm_gain = jnp.clip(1.0 + 0.18 * jax.random.normal(streams_of[1], (PAIR,), jnp.float32), 0.1, 1.9)
    norm_bias = normal_values(streams_of[2], (PAIR,), 0.5, 3.0, (), jnp.float32)
    left_weight = normal_values(streams_of[3], (PAIR, 2 * HIDDEN_SIZE), PAIR ** -0.5, 0.5)
    right_weight = normal_values(streams_of[4], (PAIR, 2 * HIDDEN_SIZE), PAIR ** -0.5, 0.5)
    gate_weight = normal_values(streams_of[5], (PAIR, PAIR), PAIR ** -0.5, 0.5)
    out_gain = jnp.clip(1.0 + 0.18 * jax.random.normal(streams_of[6], (HIDDEN_SIZE,), jnp.float32), 0.1, 1.9)
    out_bias = normal_values(streams_of[7], (HIDDEN_SIZE,), 0.5, 3.0, (), jnp.float32)
    out_weight = normal_values(streams_of[8], (HIDDEN_SIZE, PAIR), HIDDEN_SIZE ** -0.5, 0.5)
    return {"pair": pair, "norm_gain": norm_gain, "norm_bias": norm_bias, "left_weight": left_weight, "right_weight": right_weight, "gate_weight": gate_weight, "out_gain": out_gain, "out_bias": out_bias, "out_weight": out_weight}


def layer_norm(values, gain, bias):
    average = lax.optimization_barrier(jnp.mean(values, axis=-1, keepdims=True))
    centred = values - average
    variance = lax.optimization_barrier(jnp.mean(centred * centred, axis=-1, keepdims=True))
    return centred * lax.rsqrt(variance + 1e-05) * gain + bias

def reference(pair, norm_gain, norm_bias, left_weight, right_weight, gate_weight, out_gain, out_bias, out_weight):
    pieces = pair.reshape(N_ROW, TOK_ROW, TOKENS, PAIR)

    def project(block):
        normed = layer_norm(block.astype(jnp.float32), norm_gain, norm_bias).astype(jnp.bfloat16)
        flat = normed.reshape(TOK_ROW * TOKENS, PAIR)
        left_proj = jnp.dot(flat, left_weight, preferred_element_type=jnp.float32)
        right_proj = jnp.dot(flat, right_weight, preferred_element_type=jnp.float32)
        left = (jax.nn.sigmoid(left_proj[:, HIDDEN_SIZE:]) * left_proj[:, :HIDDEN_SIZE]).astype(jnp.bfloat16)
        right = (jax.nn.sigmoid(right_proj[:, HIDDEN_SIZE:]) * right_proj[:, :HIDDEN_SIZE]).astype(jnp.bfloat16)
        gate = jax.nn.sigmoid(jnp.dot(flat, gate_weight, preferred_element_type=jnp.float32)).astype(jnp.bfloat16)
        return (left.reshape(TOK_ROW, TOKENS, HIDDEN_SIZE), right.reshape(TOK_ROW, TOKENS, HIDDEN_SIZE), gate.reshape(TOK_ROW, TOKENS, PAIR))
    left, right, gate = lax.map(project, pieces)
    left_t = jnp.transpose(left.reshape(TOKENS, TOKENS, HIDDEN_SIZE), (2, 0, 1))
    right_t = jnp.transpose(right.reshape(TOKENS, TOKENS, HIDDEN_SIZE), (2, 0, 1))

    def channel(operands):
        left_h, right_h = operands
        total = jnp.dot(left_h.astype(jnp.float32).T, right_h.astype(jnp.float32), precision=lax.Precision.HIGHEST, preferred_element_type=jnp.float32)
        return total.astype(jnp.bfloat16)
    product = lax.map(channel, (left_t, right_t))
    product_rows = jnp.transpose(product, (1, 2, 0)).reshape(N_ROW, TOK_ROW, TOKENS, HIDDEN_SIZE)

    def finish(operands):
        row_block, gate_block = operands
        normed_out = layer_norm(row_block.astype(jnp.float32), out_gain, out_bias).astype(jnp.bfloat16)
        projected = jnp.dot(normed_out.reshape(TOK_ROW * TOKENS, HIDDEN_SIZE), out_weight, preferred_element_type=jnp.float32)
        gated = gate_block.reshape(TOK_ROW * TOKENS, PAIR).astype(jnp.float32) * projected
        return gated.astype(jnp.bfloat16).reshape(TOK_ROW, TOKENS, PAIR)
    update = lax.map(finish, (product_rows, gate))
    return update.reshape(TOKENS, TOKENS, PAIR)
```

```python
import functools

import jax
import jax.numpy as jnp
from jax import lax
from jax.experimental import pallas as pl
from jax.experimental.pallas import tpu as pltpu
from jax.sharding import PartitionSpec as P


def body(
    pair,
    norm_gain,
    norm_bias,
    left_weight,
    right_weight,
    gate_weight,
    out_gain,
    out_bias,
    out_weight,
):
    hidden = out_gain.shape[0]
    values = pair.astype(jnp.float32)
    average = jnp.mean(values, axis=-1, keepdims=True)
    centred = values - average
    variance = jnp.mean(centred * centred, axis=-1, keepdims=True)
    normed = (centred * lax.rsqrt(variance + 1e-05) * norm_gain + norm_bias).astype(jnp.bfloat16)

    def branch(weight):
        projected = jnp.einsum("kic,cd->dki", normed, weight, preferred_element_type=jnp.float32)
        return (jax.nn.sigmoid(projected[hidden:]) * projected[:hidden]).astype(jnp.bfloat16)

    left = branch(left_weight)
    right = branch(right_weight)
    left_mine, right_mine = (
        lax.all_to_all(left, "row", split_axis=0, concat_axis=1, tiled=True),
        lax.all_to_all(right, "row", split_axis=0, concat_axis=1, tiled=True),
    )
    gate = jax.nn.sigmoid(
        jnp.einsum("kic,cd->kid", normed, gate_weight, preferred_element_type=jnp.float32)
    ).astype(jnp.bfloat16)
    product = jnp.einsum(
        "hki,hkj->hij",
        lax.all_gather(left_mine, "col", axis=2, tiled=True),
        right_mine,
        preferred_element_type=jnp.float32,
    ).astype(jnp.bfloat16)
    returned = lax.all_to_all(product, "row", split_axis=1, concat_axis=0, tiled=True)
    stats_in = returned.astype(jnp.float32)
    out_average = jnp.mean(stats_in, axis=0, keepdims=True)
    out_centred = stats_in - out_average
    out_variance = jnp.mean(out_centred * out_centred, axis=0, keepdims=True)
    normed_out = (
        out_centred * lax.rsqrt(out_variance + 1e-05) * out_gain[:, None, None]
        + out_bias[:, None, None]
    ).astype(jnp.bfloat16)
    projected_out = jnp.einsum(
        "hij,hd->ijd", normed_out, out_weight, preferred_element_type=jnp.float32
    )
    return (gate.astype(jnp.float32) * projected_out).astype(jnp.bfloat16)


MESH = pl.DeviceIdType.MESH
CHUNKS = 2


def sigmoid(x):
    return 0.5 * jnp.tanh(0.5 * x) + 0.5


def kernel(
    rows,
    cols,
    pair_ref,
    norm_gain_ref,
    norm_bias_ref,
    left_ref,
    right_ref,
    gate_weight_ref,
    out_gain_ref,
    out_bias_ref,
    out_weight_ref,
    out_ref,
    normed,
    weights,
    staged,
    operands_out,
    operands_in,
    product_out,
    product_in,
    centred,
    gate,
    send_sem,
    recv_sem,
    send_back_sem,
    recv_back_sem,
):
    tok_row, tok_col, pair = pair_ref.shape
    hidden = out_gain_ref.shape[1]
    devices = rows * cols
    turns = hidden // devices
    per = turns // CHUNKS
    part = per * devices
    tokens = rows * tok_row
    row, col = lax.axis_index("row"), lax.axis_index("col")
    me = col * rows + row

    def others(one):
        def step(offset, carry):
            other = lax.rem(me + offset, devices)
            one(other, lax.rem(other, rows), lax.div(other, rows))
            return carry

        lax.fori_loop(1, devices, step, 0)

    barrier = pltpu.get_barrier_semaphore()
    others(
        lambda other, r, c: pl.semaphore_signal(
            barrier, inc=1, device_id={"row": r, "col": c}, device_id_type=MESH
        )
    )

    gain, bias = norm_gain_ref[...], norm_bias_ref[...]
    step_rows = 4
    for k in range(0, tok_row, step_rows):
        x = pair_ref[k : k + step_rows].reshape(step_rows * tok_col, pair).astype(jnp.float32)
        average = jnp.mean(x, axis=-1, keepdims=True)
        x = x - average
        variance = jnp.mean(x * x, axis=-1, keepdims=True)
        normed[k * tok_col : (k + step_rows) * tok_col] = (
            x * lax.rsqrt(variance + 1e-05) * gain + bias
        ).astype(jnp.bfloat16)

    for side, ref in enumerate((left_ref, right_ref)):
        turned = ref[...].astype(jnp.float32).T.astype(jnp.bfloat16)
        for m in range(CHUNKS):
            for half in range(2):
                weights[m, (2 * side + half) * part : (2 * side + half + 1) * part] = turned[
                    half * hidden + m * part : half * hidden + (m + 1) * part
                ]

    def operand_copy(m, other, r, c, slot):
        sc, sr = slot
        return pltpu.make_async_remote_copy(
            src_ref=operands_out.at[pl.ds(m * per, per), other],
            dst_ref=operands_in.at[pl.ds(m * per, per), sc, sr],
            send_sem=send_sem.at[m, other],
            recv_sem=recv_sem.at[m, sc * rows + sr],
            device_id={"row": r, "col": c},
            device_id_type=MESH,
        )

    def product_copy(m, other, r, c, slot):
        return pltpu.make_async_remote_copy(
            src_ref=product_out.at[pl.ds(m * per, per), c, r],
            dst_ref=product_in.at[pl.ds(m * per, per), slot],
            send_sem=send_back_sem.at[m, other],
            recv_sem=recv_back_sem.at[m, slot],
            device_id={"row": r, "col": c},
            device_id_type=MESH,
        )

    for m in range(CHUNKS):
        for k in range(0, tok_row, step_rows):
            projected = lax.dot_general(
                weights[m],
                normed[k * tok_col : (k + step_rows) * tok_col],
                (((1,), (1,)), ((), ())),
                preferred_element_type=jnp.float32,
            )
            for side in range(2):
                values = projected[2 * side * part : (2 * side + 1) * part]
                gates = projected[(2 * side + 1) * part : (2 * side + 2) * part]
                gated = sigmoid(gates) * values
                for kk in range(step_rows):
                    staged[side, :, k + kk, :] = gated[:, kk * tok_col : (kk + 1) * tok_col]
        for side in range(2):
            for t in range(per):
                operands_out[m * per + t, :, side] = staged[
                    side, t * devices : (t + 1) * devices
                ].astype(jnp.bfloat16)
        if m == 0:
            pl.semaphore_wait(barrier, devices - 1)
        others(lambda other, r, c: operand_copy(m, other, r, c, (col, row)).start())
        for t in range(per):
            q = m * per + t
            operands_in[q, col, row] = operands_out[q, me]

    for k in range(0, tok_row, step_rows):
        gate[k * tok_col : (k + step_rows) * tok_col] = sigmoid(
            jnp.dot(
                normed[k * tok_col : (k + step_rows) * tok_col],
                gate_weight_ref[...],
                preferred_element_type=jnp.float32,
            )
        ).astype(jnp.bfloat16)

    for m in range(CHUNKS):
        others(lambda other, r, c: operand_copy(m, other, r, c, (c, r)).wait_recv())
        for t in range(per):
            q = m * per + t
            left, right = (
                jnp.concatenate(
                    [operands_in[q, c, :, side].reshape(tokens, tok_col) for c in range(cols)],
                    axis=1,
                )
                for side in range(2)
            )
            product = lax.dot_general(
                left, right, (((0,), (0,)), ((), ())), preferred_element_type=jnp.float32
            ).astype(jnp.bfloat16)
            for c in range(cols):
                product_out[q, c] = product[:, c * tok_col : (c + 1) * tok_col].reshape(
                    rows, tok_row, tok_col
                )
        others(lambda other, r, c: product_copy(m, other, r, c, me).start())
        for t in range(per):
            q = m * per + t
            product_in[q, me] = product_out[q, col, row]

    def across(ref):
        return jnp.broadcast_to(ref[...], (tok_col, hidden)).T

    out_gain, out_bias = across(out_gain_ref), across(out_bias_ref)
    for m in range(CHUNKS):
        others(lambda other, r, c: product_copy(m, other, r, c, other).wait_recv())

    total = jnp.zeros((tok_row, tok_col), jnp.float32)
    for q in range(turns):
        total += jnp.sum(product_in[q].astype(jnp.float32), axis=0)
    average = total * (1.0 / hidden)
    squares = jnp.zeros((tok_row, tok_col), jnp.float32)
    for q in range(turns):
        x = product_in[q].astype(jnp.float32) - average
        squares += jnp.sum(x * x, axis=0)
        centred[q * devices : (q + 1) * devices] = x
    scale = lax.rsqrt(squares * (1.0 / hidden) + 1e-05)
    for i in range(tok_row):
        x = centred[:, i, :] * scale[i : i + 1] * out_gain + out_bias
        projected = lax.dot_general(
            x.astype(jnp.bfloat16),
            out_weight_ref[...],
            (((0,), (0,)), ((), ())),
            preferred_element_type=jnp.float32,
        )
        gates = gate[i * tok_col : (i + 1) * tok_col].astype(jnp.float32)
        out_ref[i] = (gates * projected).astype(jnp.bfloat16)

    for m in range(CHUNKS):
        others(lambda other, r, c: operand_copy(m, other, r, c, (c, r)).wait_send())
        others(lambda other, r, c: product_copy(m, other, r, c, other).wait_send())


def fused(rows, cols, pair, norm_gain, norm_bias, left_weight, right_weight, gate_weight, out_gain, out_bias, out_weight):
    tok_row, tok_col, channels = pair.shape
    hidden = out_gain.shape[0]
    devices = rows * cols
    turns = hidden // devices
    part = hidden // CHUNKS
    bf16, f32 = jnp.bfloat16, jnp.float32
    return pl.pallas_call(
        functools.partial(kernel, rows, cols),
        out_shape=jax.ShapeDtypeStruct(pair.shape, bf16),
        in_specs=[pl.BlockSpec(memory_space=pltpu.VMEM)] * 9,
        out_specs=pl.BlockSpec(memory_space=pltpu.VMEM),
        scratch_shapes=[
            pltpu.VMEM((tok_row * tok_col, channels), bf16),
            pltpu.VMEM((CHUNKS, 4 * part, channels), bf16),
            pltpu.VMEM((2, part, tok_row, tok_col), f32),
            pltpu.VMEM((turns, devices, 2, tok_row, tok_col), bf16),
            pltpu.VMEM((turns, cols, rows, 2, tok_row, tok_col), bf16),
            pltpu.VMEM((turns, cols, rows, tok_row, tok_col), bf16),
            pltpu.VMEM((turns, devices, tok_row, tok_col), bf16),
            pltpu.VMEM((hidden, tok_row, tok_col), f32),
            pltpu.VMEM((tok_row * tok_col, channels), bf16),
            pltpu.SemaphoreType.DMA((CHUNKS, devices)),
            pltpu.SemaphoreType.DMA((CHUNKS, devices)),
            pltpu.SemaphoreType.DMA((CHUNKS, devices)),
            pltpu.SemaphoreType.DMA((CHUNKS, devices)),
        ],
        compiler_params=pltpu.CompilerParams(
            collective_id=0, has_side_effects=True, vmem_limit_bytes=40 * 2**20
        ),
    )(
        pair,
        norm_gain[None],
        norm_bias[None],
        left_weight,
        right_weight,
        gate_weight,
        out_gain[None],
        out_bias[None],
        out_weight,
    )


def solution(mesh):
    in_specs = (P(("crop", "row"), "col", None), P(), P(), P(), P(), P(), P(), P(), P())
    out_specs = P(("crop", "row"), "col", None)
    rows, cols = mesh.shape["row"], mesh.shape["col"]

    def local(pair, norm_gain, *rest):
        hidden = rest[4].shape[0]
        if hidden % (rows * cols * CHUNKS) == 0:
            return fused(rows, cols, pair, norm_gain, *rest)
        return body(pair, norm_gain, *rest)

    return jax.shard_map(local, mesh=mesh, in_specs=in_specs, out_specs=out_specs, check_vma=False)
```

```python
import functools

import jax
import jax.numpy as jnp
from jax import lax
from jax.experimental import pallas as pl
from jax.experimental.pallas import tpu as pltpu
from jax.sharding import PartitionSpec as P


def body(
    pair,
    norm_gain,
    norm_bias,
    left_weight,
    right_weight,
    gate_weight,
    out_gain,
    out_bias,
    out_weight,
):
    hidden = out_gain.shape[0]
    values = pair.astype(jnp.float32)
    average = jnp.mean(values, axis=-1, keepdims=True)
    centred = values - average
    variance = jnp.mean(centred * centred, axis=-1, keepdims=True)
    normed = (centred * lax.rsqrt(variance + 1e-05) * norm_gain + norm_bias).astype(jnp.bfloat16)

    def branch(weight):
        projected = jnp.einsum("kic,cd->dki", normed, weight, preferred_element_type=jnp.float32)
        return (jax.nn.sigmoid(projected[hidden:]) * projected[:hidden]).astype(jnp.bfloat16)

    left = branch(left_weight)
    right = branch(right_weight)
    left_mine, right_mine = (
        lax.all_to_all(left, "row", split_axis=0, concat_axis=1, tiled=True),
        lax.all_to_all(right, "row", split_axis=0, concat_axis=1, tiled=True),
    )
    gate = jax.nn.sigmoid(
        jnp.einsum("kic,cd->kid", normed, gate_weight, preferred_element_type=jnp.float32)
    ).astype(jnp.bfloat16)
    product = jnp.einsum(
        "hki,hkj->hij",
        lax.all_gather(left_mine, "col", axis=2, tiled=True),
        right_mine,
        preferred_element_type=jnp.float32,
    ).astype(jnp.bfloat16)
    returned = lax.all_to_all(product, "row", split_axis=1, concat_axis=0, tiled=True)
    stats_in = returned.astype(jnp.float32)
    out_average = jnp.mean(stats_in, axis=0, keepdims=True)
    out_centred = stats_in - out_average
    out_variance = jnp.mean(out_centred * out_centred, axis=0, keepdims=True)
    normed_out = (
        out_centred * lax.rsqrt(out_variance + 1e-05) * out_gain[:, None, None]
        + out_bias[:, None, None]
    ).astype(jnp.bfloat16)
    projected_out = jnp.einsum(
        "hij,hd->ijd", normed_out, out_weight, preferred_element_type=jnp.float32
    )
    return (gate.astype(jnp.float32) * projected_out).astype(jnp.bfloat16)


MESH = pl.DeviceIdType.MESH
CHUNKS = 4
UNROLL = 1
PACED = False
HALVES = 2


def sigmoid(x):
    return 0.5 * jnp.tanh(0.5 * x) + 0.5


def kernel(rows, cols, *refs):
    arguments, out_ref = refs[:9], refs[9]
    held = refs[10:19]
    (
        normed,
        weights,
        staged,
        operands_out,
        operands_in,
        product_out,
        product_in,
        centred,
        gate,
        fetch_sem,
        send_sem,
        recv_sem,
        send_back_sem,
        recv_back_sem,
    ) = refs[19:]
    fetches = [
        pltpu.make_async_copy(source, target, fetch_sem.at[n])
        for n, (source, target) in enumerate(zip(arguments, held))
    ]
    for fetch in fetches:
        fetch.start()
    (
        pair_ref,
        norm_gain_ref,
        norm_bias_ref,
        left_ref,
        right_ref,
        gate_weight_ref,
        out_gain_ref,
        out_bias_ref,
        out_weight_ref,
    ) = held
    tok_row, tok_col, pair = pair_ref.shape
    hidden = out_gain_ref.shape[1]
    half_rows = rows // HALVES
    members = half_rows * cols
    turns = hidden // members
    per = turns // CHUNKS
    part = per * members
    half_tokens = half_rows * tok_row
    row, col = lax.axis_index("row"), lax.axis_index("col")
    half, half_row = lax.div(row, half_rows), lax.rem(row, half_rows)
    me = col * half_rows + half_row

    def near(one):
        def step(offset, carry):
            other = lax.rem(me + offset, members)
            one(half, other, lax.rem(other, half_rows), lax.div(other, half_rows))
            return carry

        lax.fori_loop(1, members, step, 0, unroll=UNROLL)

    def far(one):
        for away in range(1, HALVES):

            def step(offset, carry):
                other = lax.rem(me + offset, members)
                one(
                    lax.rem(half + away, HALVES),
                    other,
                    lax.rem(other, half_rows),
                    lax.div(other, half_rows),
                )
                return carry

            lax.fori_loop(0, members, step, 0, unroll=UNROLL)

    def everyone(one):
        far(one)
        near(one)

    def place(h, r, c):
        return {"row": h * half_rows + r, "col": c}

    barrier = pltpu.get_barrier_semaphore()
    everyone(
        lambda h, other, r, c: pl.semaphore_signal(
            barrier, inc=1, device_id=place(h, r, c), device_id_type=MESH
        )
    )
    for fetch in fetches:
        fetch.wait()

    gain, bias = norm_gain_ref[...], norm_bias_ref[...]
    step_rows = 4
    for k in range(0, tok_row, step_rows):
        x = pair_ref[k : k + step_rows].reshape(step_rows * tok_col, pair).astype(jnp.float32)
        average = jnp.mean(x, axis=-1, keepdims=True)
        x = x - average
        variance = jnp.mean(x * x, axis=-1, keepdims=True)
        normed[k * tok_col : (k + step_rows) * tok_col] = (
            x * lax.rsqrt(variance + 1e-05) * gain + bias
        ).astype(jnp.bfloat16)

    for side, ref in enumerate((left_ref, right_ref)):
        turned = ref[...].astype(jnp.float32).T.astype(jnp.bfloat16)
        for m in range(CHUNKS):
            for piece in range(2):
                weights[m, (2 * side + piece) * part : (2 * side + piece + 1) * part] = turned[
                    piece * hidden + m * part : piece * hidden + (m + 1) * part
                ]

    def operand_copy(m, h, other, r, c, slot):
        return pltpu.make_async_remote_copy(
            src_ref=operands_out.at[pl.ds(m * per, per), other],
            dst_ref=operands_in.at[pl.ds(m * per, per), slot],
            send_sem=send_sem.at[m],
            recv_sem=recv_sem.at[m],
            device_id=place(h, r, c),
            device_id_type=MESH,
        )

    def product_copy(m, h, other, r, c, slot):
        return pltpu.make_async_remote_copy(
            src_ref=product_out.at[pl.ds(m * per, per), c, h * half_rows + r],
            dst_ref=product_in.at[pl.ds(m * per, per), slot],
            send_sem=send_back_sem.at[m],
            recv_sem=recv_back_sem.at[m],
            device_id=place(h, r, c),
            device_id_type=MESH,
        )

    def arrived(ref, m, blocks, sem):
        all_blocks = ref.at[pl.ds(m * per, per), pl.ds(0, blocks)]
        pltpu.make_async_copy(all_blocks, all_blocks, sem.at[m]).wait()

    def project(m):
        for k in range(0, tok_row, step_rows):
            projected = lax.dot_general(
                weights[m],
                normed[k * tok_col : (k + step_rows) * tok_col],
                (((1,), (1,)), ((), ())),
                preferred_element_type=jnp.float32,
            )
            for side in range(2):
                values = projected[2 * side * part : (2 * side + 1) * part]
                gates = projected[(2 * side + 1) * part : (2 * side + 2) * part]
                gated = sigmoid(gates) * values
                for kk in range(step_rows):
                    staged[side, :, k + kk, :] = gated[:, kk * tok_col : (kk + 1) * tok_col]
        for side in range(2):
            for t in range(per):
                operands_out[m * per + t, :, side] = staged[
                    side, t * members : (t + 1) * members
                ].astype(jnp.bfloat16)

    def send_operands(m):
        near(lambda h, other, r, c: operand_copy(m, h, other, r, c, me).start())
        for t in range(per):
            q = m * per + t
            operands_in[q, me] = operands_out[q, me]

    project(0)
    pl.semaphore_wait(barrier, HALVES * members - 1)
    send_operands(0)
    if not PACED:
        for m in range(1, CHUNKS):
            project(m)
            send_operands(m)
    for m in range(CHUNKS):
        if PACED and m + 1 < CHUNKS:
            project(m + 1)
        arrived(operands_in, m, members - 1, recv_sem)
        if PACED and m + 1 < CHUNKS:
            send_operands(m + 1)
        for t in range(per):
            q = m * per + t
            left, right = (
                jnp.concatenate(
                    [
                        operands_in[q, c * half_rows : (c + 1) * half_rows, side].reshape(
                            half_tokens, tok_col
                        )
                        for c in range(cols)
                    ],
                    axis=1,
                )
                for side in range(2)
            )
            product = lax.dot_general(
                left, right, (((0,), (0,)), ((), ())), preferred_element_type=jnp.float32
            ).astype(jnp.bfloat16)
            for c in range(cols):
                product_out[q, c] = product[:, c * tok_col : (c + 1) * tok_col].reshape(
                    rows, tok_row, tok_col
                )
        everyone(lambda h, other, r, c: product_copy(m, h, other, r, c, half * members + me).start())
        for t in range(per):
            q = m * per + t
            product_in[q, half * members + me] = product_out[q, col, row]

    for k in range(0, tok_row, step_rows):
        gate[k * tok_col : (k + step_rows) * tok_col] = sigmoid(
            jnp.dot(
                normed[k * tok_col : (k + step_rows) * tok_col],
                gate_weight_ref[...],
                preferred_element_type=jnp.float32,
            )
        ).astype(jnp.bfloat16)

    def across(ref):
        return jnp.broadcast_to(ref[...], (tok_col, hidden)).T

    out_gain, out_bias = across(out_gain_ref), across(out_bias_ref)
    averages, squares = [], []
    for m in range(CHUNKS):
        arrived(product_in, m, HALVES * members - 1, recv_back_sem)
        total = jnp.zeros((tok_row, tok_col), jnp.float32)
        for q in range(m * per, (m + 1) * per):
            x = product_in[q, :members].astype(jnp.float32)
            for h in range(1, HALVES):
                x += product_in[q, h * members : (h + 1) * members].astype(jnp.float32)
            centred[q * members : (q + 1) * members] = x
            total += jnp.sum(x, axis=0)
        average = total * (1.0 / part)
        square = jnp.zeros((tok_row, tok_col), jnp.float32)
        for q in range(m * per, (m + 1) * per):
            x = centred[q * members : (q + 1) * members] - average
            square += jnp.sum(x * x, axis=0)
        averages.append(average)
        squares.append(square)
    average = sum(averages) * (1.0 / CHUNKS)
    square = sum(squares)
    for one in averages:
        square += part * (one - average) * (one - average)
    scale = lax.rsqrt(square * (1.0 / hidden) + 1e-05)
    for i in range(tok_row):
        x = (centred[:, i, :] - average[i : i + 1]) * scale[i : i + 1] * out_gain + out_bias
        projected = lax.dot_general(
            x.astype(jnp.bfloat16),
            out_weight_ref[...],
            (((0,), (0,)), ((), ())),
            preferred_element_type=jnp.float32,
        )
        gates = gate[i * tok_col : (i + 1) * tok_col].astype(jnp.float32)
        out_ref[i] = (gates * projected).astype(jnp.bfloat16)

    for m in range(CHUNKS):
        arrived(operands_in, m, members - 1, send_sem)
        arrived(product_in, m, HALVES * members - 1, send_back_sem)


def fused(rows, cols, *arguments):
    arguments = [pltpu.with_memory_space_constraint(a[None] if a.ndim == 1 else a, pltpu.HBM) for a in arguments]
    tok_row, tok_col, channels = arguments[0].shape
    hidden = arguments[6].shape[1]
    members = rows * cols // HALVES
    turns = hidden // members
    part = hidden // CHUNKS
    bf16, f32 = jnp.bfloat16, jnp.float32
    dma = pltpu.SemaphoreType.DMA
    return pl.pallas_call(
        functools.partial(kernel, rows, cols),
        out_shape=jax.ShapeDtypeStruct(arguments[0].shape, bf16),
        in_specs=[pl.BlockSpec(memory_space=pltpu.HBM)] * 9,
        out_specs=pl.BlockSpec(memory_space=pltpu.VMEM),
        scratch_shapes=[pltpu.VMEM(a.shape, a.dtype) for a in arguments]
        + [
            pltpu.VMEM((tok_row * tok_col, channels), bf16),
            pltpu.VMEM((CHUNKS, 4 * part, channels), bf16),
            pltpu.VMEM((2, part, tok_row, tok_col), f32),
            pltpu.VMEM((turns, members, 2, tok_row, tok_col), bf16),
            pltpu.VMEM((turns, members, 2, tok_row, tok_col), bf16),
            pltpu.VMEM((turns, cols, rows, tok_row, tok_col), bf16),
            pltpu.VMEM((turns, HALVES * members, tok_row, tok_col), bf16),
            pltpu.VMEM((hidden, tok_row, tok_col), f32),
            pltpu.VMEM((tok_row * tok_col, channels), bf16),
            dma((9,)),
            dma((CHUNKS,)),
            dma((CHUNKS,)),
            dma((CHUNKS,)),
            dma((CHUNKS,)),
        ],
        compiler_params=pltpu.CompilerParams(
            collective_id=0, has_side_effects=True, vmem_limit_bytes=40 * 2**20
        ),
    )(*arguments)


def solution(mesh):
    in_specs = (P(("crop", "row"), "col", None), P(), P(), P(), P(), P(), P(), P(), P())
    out_specs = P(("crop", "row"), "col", None)
    rows, cols = mesh.shape["row"], mesh.shape["col"]

    def local(*arguments):
        channels = arguments[6].shape[0] * HALVES
        if rows % HALVES == 0 and channels % (rows * cols * CHUNKS) == 0:
            return fused(rows, cols, *arguments)
        return body(*arguments)

    return jax.shard_map(local, mesh=mesh, in_specs=in_specs, out_specs=out_specs, check_vma=False)
```

```python
import functools

import jax
import jax.numpy as jnp
from jax import lax
from jax.experimental import pallas as pl
from jax.experimental.pallas import tpu as pltpu
from jax.sharding import PartitionSpec as P


def body(
    pair,
    norm_gain,
    norm_bias,
    left_weight,
    right_weight,
    gate_weight,
    out_gain,
    out_bias,
    out_weight,
):
    hidden = out_gain.shape[0]
    values = pair.astype(jnp.float32)
    average = jnp.mean(values, axis=-1, keepdims=True)
    centred = values - average
    variance = jnp.mean(centred * centred, axis=-1, keepdims=True)
    normed = (centred * lax.rsqrt(variance + 1e-05) * norm_gain + norm_bias).astype(jnp.bfloat16)

    def branch(weight):
        projected = jnp.einsum("kic,cd->dki", normed, weight, preferred_element_type=jnp.float32)
        return (jax.nn.sigmoid(projected[hidden:]) * projected[:hidden]).astype(jnp.bfloat16)

    left = branch(left_weight)
    right = branch(right_weight)
    left_mine, right_mine = (
        lax.all_to_all(left, "row", split_axis=0, concat_axis=1, tiled=True),
        lax.all_to_all(right, "row", split_axis=0, concat_axis=1, tiled=True),
    )
    gate = jax.nn.sigmoid(
        jnp.einsum("kic,cd->kid", normed, gate_weight, preferred_element_type=jnp.float32)
    ).astype(jnp.bfloat16)
    product = jnp.einsum(
        "hki,hkj->hij",
        lax.all_gather(left_mine, "col", axis=2, tiled=True),
        right_mine,
        preferred_element_type=jnp.float32,
    ).astype(jnp.bfloat16)
    returned = lax.all_to_all(product, "row", split_axis=1, concat_axis=0, tiled=True)
    stats_in = returned.astype(jnp.float32)
    out_average = jnp.mean(stats_in, axis=0, keepdims=True)
    out_centred = stats_in - out_average
    out_variance = jnp.mean(out_centred * out_centred, axis=0, keepdims=True)
    normed_out = (
        out_centred * lax.rsqrt(out_variance + 1e-05) * out_gain[:, None, None]
        + out_bias[:, None, None]
    ).astype(jnp.bfloat16)
    projected_out = jnp.einsum(
        "hij,hd->ijd", normed_out, out_weight, preferred_element_type=jnp.float32
    )
    return (gate.astype(jnp.float32) * projected_out).astype(jnp.bfloat16)


MESH = pl.DeviceIdType.MESH
CHUNKS = 8
AHEAD = 4
HALVES = 2


def sigmoid(x):
    return 0.5 * jnp.tanh(0.5 * x) + 0.5


def kernel(rows, cols, *refs):
    arguments, out_ref = refs[:9], refs[9]
    held = refs[10:19]
    (
        normed,
        weights,
        staged,
        operands_out,
        operands_in,
        product_out,
        product_in,
        centred,
        gate,
        fetch_sem,
        send_sem,
        recv_sem,
        send_back_sem,
        recv_back_sem,
    ) = refs[19:]
    fetches = [
        pltpu.make_async_copy(source, target, fetch_sem.at[n])
        for n, (source, target) in enumerate(zip(arguments, held))
    ]
    for fetch in fetches:
        fetch.start()
    (
        pair_ref,
        norm_gain_ref,
        norm_bias_ref,
        left_ref,
        right_ref,
        gate_weight_ref,
        out_gain_ref,
        out_bias_ref,
        out_weight_ref,
    ) = held
    tok_row, tok_col, pair = pair_ref.shape
    hidden = out_gain_ref.shape[1]
    half_rows = rows // HALVES
    members = half_rows * cols
    turns = hidden // members
    per = turns // CHUNKS
    part = per * members
    half_tokens = half_rows * tok_row
    row, col = lax.axis_index("row"), lax.axis_index("col")
    half, half_row = lax.div(row, half_rows), lax.rem(row, half_rows)
    me = col * half_rows + half_row

    def near(one):
        def step(offset, carry):
            other = lax.rem(me + offset, members)
            one(half, other, lax.rem(other, half_rows), lax.div(other, half_rows))
            return carry

        lax.fori_loop(1, members, step, 0)

    def far(one):
        for away in range(1, HALVES):

            def step(offset, carry):
                other = lax.rem(me + offset, members)
                one(
                    lax.rem(half + away, HALVES),
                    other,
                    lax.rem(other, half_rows),
                    lax.div(other, half_rows),
                )
                return carry

            lax.fori_loop(0, members, step, 0)

    def everyone(one):
        far(one)
        near(one)

    def place(h, r, c):
        return {"row": h * half_rows + r, "col": c}

    barrier = pltpu.get_barrier_semaphore()
    everyone(
        lambda h, other, r, c: pl.semaphore_signal(
            barrier, inc=1, device_id=place(h, r, c), device_id_type=MESH
        )
    )
    for fetch in fetches:
        fetch.wait()

    gain, bias = norm_gain_ref[...], norm_bias_ref[...]
    step_rows = 4
    for k in range(0, tok_row, step_rows):
        x = pair_ref[k : k + step_rows].reshape(step_rows * tok_col, pair).astype(jnp.float32)
        average = jnp.mean(x, axis=-1, keepdims=True)
        x = x - average
        variance = jnp.mean(x * x, axis=-1, keepdims=True)
        normed[k * tok_col : (k + step_rows) * tok_col] = (
            x * lax.rsqrt(variance + 1e-05) * gain + bias
        ).astype(jnp.bfloat16)

    for side, ref in enumerate((left_ref, right_ref)):
        turned = ref[...].astype(jnp.float32).T.astype(jnp.bfloat16)
        for m in range(CHUNKS):
            for piece in range(2):
                weights[m, (2 * side + piece) * part : (2 * side + piece + 1) * part] = turned[
                    piece * hidden + m * part : piece * hidden + (m + 1) * part
                ]

    def operand_copy(m, h, other, r, c, slot):
        return pltpu.make_async_remote_copy(
            src_ref=operands_out.at[pl.ds(m * per, per), other],
            dst_ref=operands_in.at[pl.ds(m * per, per), slot],
            send_sem=send_sem.at[m],
            recv_sem=recv_sem.at[m],
            device_id=place(h, r, c),
            device_id_type=MESH,
        )

    def product_copy(m, h, other, r, c, slot):
        return pltpu.make_async_remote_copy(
            src_ref=product_out.at[pl.ds(m * per, per), c, h * half_rows + r],
            dst_ref=product_in.at[pl.ds(m * per, per), slot],
            send_sem=send_back_sem.at[m],
            recv_sem=recv_back_sem.at[m],
            device_id=place(h, r, c),
            device_id_type=MESH,
        )

    def arrived(ref, m, blocks, sem):
        all_blocks = ref.at[pl.ds(m * per, per), pl.ds(0, blocks)]
        pltpu.make_async_copy(all_blocks, all_blocks, sem.at[m]).wait()

    def project(m):
        for k in range(0, tok_row, step_rows):
            projected = lax.dot_general(
                weights[m],
                normed[k * tok_col : (k + step_rows) * tok_col],
                (((1,), (1,)), ((), ())),
                preferred_element_type=jnp.float32,
            )
            for side in range(2):
                values = projected[2 * side * part : (2 * side + 1) * part]
                gates = projected[(2 * side + 1) * part : (2 * side + 2) * part]
                gated = sigmoid(gates) * values
                for kk in range(step_rows):
                    staged[side, :, k + kk, :] = gated[:, kk * tok_col : (kk + 1) * tok_col]
        for side in range(2):
            for t in range(per):
                operands_out[m * per + t, :, side] = staged[
                    side, t * members : (t + 1) * members
                ].astype(jnp.bfloat16)

    def send_operands(m):
        near(lambda h, other, r, c: operand_copy(m, h, other, r, c, me).start())
        for t in range(per):
            q = m * per + t
            operands_in[q, me] = operands_out[q, me]

    for m in range(AHEAD):
        project(m)
        if m == 0:
            pl.semaphore_wait(barrier, HALVES * members - 1)
        send_operands(m)
    for m in range(CHUNKS):
        if m + AHEAD < CHUNKS:
            project(m + AHEAD)
        arrived(operands_in, m, members - 1, recv_sem)
        if m + AHEAD < CHUNKS:
            send_operands(m + AHEAD)
        for t in range(per):
            q = m * per + t
            left, right = (
                jnp.concatenate(
                    [
                        operands_in[q, c * half_rows : (c + 1) * half_rows, side].reshape(
                            half_tokens, tok_col
                        )
                        for c in range(cols)
                    ],
                    axis=1,
                )
                for side in range(2)
            )
            product = lax.dot_general(
                left, right, (((0,), (0,)), ((), ())), preferred_element_type=jnp.float32
            ).astype(jnp.bfloat16)
            for c in range(cols):
                product_out[q, c] = product[:, c * tok_col : (c + 1) * tok_col].reshape(
                    rows, tok_row, tok_col
                )
        everyone(lambda h, other, r, c: product_copy(m, h, other, r, c, half * members + me).start())
        for t in range(per):
            q = m * per + t
            product_in[q, half * members + me] = product_out[q, col, row]

    for k in range(0, tok_row, step_rows):
        gate[k * tok_col : (k + step_rows) * tok_col] = sigmoid(
            jnp.dot(
                normed[k * tok_col : (k + step_rows) * tok_col],
                gate_weight_ref[...],
                preferred_element_type=jnp.float32,
            )
        ).astype(jnp.bfloat16)

    def across(ref):
        return jnp.broadcast_to(ref[...], (tok_col, hidden)).T

    out_gain, out_bias = across(out_gain_ref), across(out_bias_ref)
    averages, squares = [], []
    for m in range(CHUNKS):
        arrived(product_in, m, HALVES * members - 1, recv_back_sem)
        total = jnp.zeros((tok_row, tok_col), jnp.float32)
        for q in range(m * per, (m + 1) * per):
            x = product_in[q, :members].astype(jnp.float32)
            for h in range(1, HALVES):
                x += product_in[q, h * members : (h + 1) * members].astype(jnp.float32)
            centred[q * members : (q + 1) * members] = x
            total += jnp.sum(x, axis=0)
        average = total * (1.0 / part)
        square = jnp.zeros((tok_row, tok_col), jnp.float32)
        for q in range(m * per, (m + 1) * per):
            x = centred[q * members : (q + 1) * members] - average
            square += jnp.sum(x * x, axis=0)
        averages.append(average)
        squares.append(square)
    average = sum(averages) * (1.0 / CHUNKS)
    square = sum(squares)
    for one in averages:
        square += part * (one - average) * (one - average)
    scale = lax.rsqrt(square * (1.0 / hidden) + 1e-05)
    for i in range(tok_row):
        x = (centred[:, i, :] - average[i : i + 1]) * scale[i : i + 1] * out_gain + out_bias
        projected = lax.dot_general(
            x.astype(jnp.bfloat16),
            out_weight_ref[...],
            (((0,), (0,)), ((), ())),
            preferred_element_type=jnp.float32,
        )
        gates = gate[i * tok_col : (i + 1) * tok_col].astype(jnp.float32)
        out_ref[i] = (gates * projected).astype(jnp.bfloat16)

    for m in range(CHUNKS):
        arrived(operands_in, m, members - 1, send_sem)
        arrived(product_in, m, HALVES * members - 1, send_back_sem)


def fused(rows, cols, *arguments):
    arguments = [pltpu.with_memory_space_constraint(a[None] if a.ndim == 1 else a, pltpu.HBM) for a in arguments]
    tok_row, tok_col, channels = arguments[0].shape
    hidden = arguments[6].shape[1]
    members = rows * cols // HALVES
    turns = hidden // members
    part = hidden // CHUNKS
    bf16, f32 = jnp.bfloat16, jnp.float32
    dma = pltpu.SemaphoreType.DMA
    return pl.pallas_call(
        functools.partial(kernel, rows, cols),
        out_shape=jax.ShapeDtypeStruct(arguments[0].shape, bf16),
        in_specs=[pl.BlockSpec(memory_space=pltpu.HBM)] * 9,
        out_specs=pl.BlockSpec(memory_space=pltpu.VMEM),
        scratch_shapes=[pltpu.VMEM(a.shape, a.dtype) for a in arguments]
        + [
            pltpu.VMEM((tok_row * tok_col, channels), bf16),
            pltpu.VMEM((CHUNKS, 4 * part, channels), bf16),
            pltpu.VMEM((2, part, tok_row, tok_col), f32),
            pltpu.VMEM((turns, members, 2, tok_row, tok_col), bf16),
            pltpu.VMEM((turns, members, 2, tok_row, tok_col), bf16),
            pltpu.VMEM((turns, cols, rows, tok_row, tok_col), bf16),
            pltpu.VMEM((turns, HALVES * members, tok_row, tok_col), bf16),
            pltpu.VMEM((hidden, tok_row, tok_col), f32),
            pltpu.VMEM((tok_row * tok_col, channels), bf16),
            dma((9,)),
            dma((CHUNKS,)),
            dma((CHUNKS,)),
            dma((CHUNKS,)),
            dma((CHUNKS,)),
        ],
        compiler_params=pltpu.CompilerParams(
            collective_id=0, has_side_effects=True, vmem_limit_bytes=40 * 2**20
        ),
    )(*arguments)


def solution(mesh):
    in_specs = (P(("crop", "row"), "col", None), P(), P(), P(), P(), P(), P(), P(), P())
    out_specs = P(("crop", "row"), "col", None)
    rows, cols = mesh.shape["row"], mesh.shape["col"]

    def local(*arguments):
        channels = arguments[6].shape[0] * HALVES
        if rows % HALVES == 0 and channels % (rows * cols * CHUNKS) == 0:
            return fused(rows, cols, *arguments)
        return body(*arguments)

    return jax.shard_map(local, mesh=mesh, in_specs=in_specs, out_specs=out_specs, check_vma=False)
```
